256 devices in a mesh: bins: 8 (over y, core), sites: 32 (over x, z).
Axes of the slice: x: 4, y: 4, z: 8, core: 2. Of those that a mesh axis runs over, the one named last changes fastest.
Arguments:
- greens: bfloat16 [4096, 8, 2048], P('sites'), may hold values from -6 to 6
- moment_rate: bfloat16 [8, 64, 64], P('bins'), may hold values from -0.09375 to 0.09375
- bin_owner: int32 [256, 64, 1], P(('bins', 'sites')), may hold values from 0 to 31; in each aligned block of 64 rows (0 to 63, 64 to 127, ..., all dimensions but the last counted through in order) at most 3 rows name the same one
- bin_local: int32 [256, 64], P(('bins', 'sites')), may hold values from 0 to 127
Outputs:
- shaking: bfloat16 [256, 8, 8, 2048], P(('bins', 'sites'))
The draws below stay inside these ranges and needn't reach their ends.
Inputs may be any that keep to these rules, and one draw needn't show every extreme that they name: `bin_owner`: among the 64 subfaults of one site no range number appears more than 3 times, and in some sites one appears exactly 3 times.
All inputs are finite; a program needn't handle non-finite values.
Results may differ from the reference program's by a relative error of at most 0.001.
Values may be sent and summed in bfloat16 or wider, within the bound.
A program may use at most 128 MiB of HBM per device.

```python
import math
import jax
import jax.numpy as jnp
import numpy as np
from jax import lax

CH = 8
NT = 2048
L = 64
TB = 32
VAR = 8
SUB = 64
BIN_DEV = 128
SITES = 256
BINS = 4096
CAPS = 3
N_SITES = 32


def with_ends(entries, stream_key, low, top_value):
    spot = [jax.random.randint(jax.random.fold_in(stream_key, axis), (), 0, length) for axis, length in enumerate(entries.shape)]
    main_axis = entries.shape.index(max(entries.shape))
    neighbour = spot[:main_axis] + [(spot[main_axis] + 1) % entries.shape[main_axis]] + spot[main_axis + 1:]
    return entries.at[tuple(spot)].set(low).at[tuple(neighbour)].set(top_value)


def shard_levels(rng, shape, cuts, least, top_value):
    level = 1.0
    for dim, parts in cuts:
        steps = jax.random.uniform(jax.random.fold_in(jax.random.fold_in(rng, 6), dim), (parts,), jnp.float32, least / len(cuts), top_value / len(cuts))
        level = level * jnp.repeat(jnp.exp(steps), shape[dim] // parts).reshape((-1,) + (1,) * (len(shape) - 1 - dim))
    return level


def assign_block(key, own, number, rows, number_of, top, most, skew):
    order = jax.random.permutation(key, number_of)
    heavy_load, ordinary = load_shares(number_of, rows * top, most, skew, True), load_shares(number_of, rows * top, most, skew, False)
    places = jnp.arange(number_of)

    def named(sizes, turn):
        used = int((sizes > 0).sum())
        fixed = max(1, used // 4)
        moved = fixed + (places - fixed + turn * (used - fixed)) % max(1, number_of - fixed)
        return jnp.zeros((number_of,), jnp.int32).at[order[jnp.where(places < fixed, places, moved)]].set(jnp.asarray(sizes, jnp.int32))

    sizes = jnp.where(number % 4 == 0, named(heavy_load, number // 4), named(ordinary, number - number // 4 - 1))
    mixed = jax.random.permutation(jax.random.fold_in(own, 3), number_of)
    source_of, taker = mixed[0:number_of // 2 * 2:2], mixed[1:number_of // 2 * 2:2]
    margin = jnp.minimum(sizes[source_of] - 1, most - sizes[taker]) // 2
    margin = jnp.where((source_of == order[0]) | (taker == order[0]) | (sizes[taker] == 0), 0, jnp.maximum(margin, 0))
    moved = jax.random.randint(jax.random.fold_in(own, 4), (number_of // 2,), 0, 1 << 20) % (margin + 1)
    sizes = sizes.at[source_of].add(-moved).at[taker].add(moved)
    labels = jnp.searchsorted(jnp.cumsum(sizes), jnp.arange(rows * top), side="right").astype(jnp.int32)
    grid = labels.reshape(top, rows).T
    grid = grid[jax.random.permutation(jax.random.fold_in(own, 1), rows)]
    turn = jax.random.randint(jax.random.fold_in(own, 2), (rows, 1), 0, top)
    return jnp.take_along_axis(grid, (jnp.arange(top)[None, :] + turn) % top, axis=1)


def load_shares(number_of, total, most, skew, full):
    loads = [(1 << 20) // math.isqrt(rank ** skew) + 1 for rank in range(1, number_of + 1)]
    largest = most if full else min(most, max(-(-total // number_of), total * loads[0] // sum(loads)))
    least = 1 if total - largest >= number_of - 1 else 0
    holding, rest = [largest] + [least] * (number_of - 1), total - largest - least * (number_of - 1)
    while rest > 0:
        candidates = [i for i in range(1, number_of) if holding[i] < largest] or [i for i in range(1, number_of) if holding[i] < most]
        mass, remaining = sum([loads[i] for i in candidates]), rest
        for i in candidates:
            addition = min(most - holding[i], max(1, remaining * loads[i] // mass), rest)
            holding[i] = holding[i] + addition
            rest = rest - addition
    return np.array(holding)


def normal_values(key, shape, deviation, bound, cuts=(), kind=jnp.bfloat16):
    values = deviation * jax.random.normal(key, shape, jnp.float32)
    if cuts:
        values = values * shard_levels(key, shape, cuts, -0.22, 0.18)
    return jnp.clip(values, -bound, bound).astype(kind)


def setup_inputs(seed: int = 0) -> dict:
    arg_keys = jax.random.split(jax.random.key(seed), 5)
    greens = normal_values(arg_keys[0], (BINS, CH, NT), 1.0, 6.0, ((0, 32),))
    moment_rate = normal_values(arg_keys[1], (VAR, SUB, L), (SUB * L) ** -0.5, 0.09375, ((0, 8),))
    bin_owner_keys = jax.random.split(jax.random.fold_in(arg_keys[2], 1), SITES * SUB // SUB)
    bin_owner_turns = jax.random.permutation(jax.random.fold_in(arg_keys[2], 3), SITES * SUB // SUB)
    bin_owner = jax.vmap(lambda own, number: assign_block(jax.random.fold_in(arg_keys[2], 2), own, number, SUB, N_SITES, 1, CAPS, 2))(bin_owner_keys, bin_owner_turns).reshape((SITES, SUB, 1))
    bin_local = with_ends(jax.random.randint(arg_keys[3], (SITES, SUB), 0, BIN_DEV), jax.random.fold_in(arg_keys[3], 1), 0, BIN_DEV - 1).astype(jnp.int32)
    return {"greens": greens, "moment_rate": moment_rate, "bin_owner": bin_owner, "bin_local": bin_local}


def kernel_table(moment):
    variations, faults, duration = moment.shape
    offsets = duration // TB + 1
    lagged = (jnp.arange(offsets)[:, None, None] * TB + jnp.arange(TB)[None, None, :]
              - jnp.arange(TB)[None, :, None])
    inside = (lagged >= 0) & (lagged < duration)
    picked = moment[:, :, jnp.clip(lagged, 0, duration - 1)]
    picked = jnp.where(inside, picked, jnp.zeros((), moment.dtype))
    return picked.transpose(2, 1, 3, 0, 4).reshape(offsets, faults, TB, variations * TB)


def stack_blocks(fetched, offsets):
    leading = fetched.ndim - 3
    faults, channels, samples = fetched.shape[leading:]
    block_count = samples // TB
    blocks = fetched.reshape(fetched.shape[:leading] + (faults, channels, block_count, TB))
    permuted = tuple(range(leading)) + (leading + 1, leading + 2, leading, leading + 3)
    blocks = jnp.transpose(blocks, permuted)
    widths = [(0, 0)] * leading + [(0, 0), (offsets - 1, 0), (0, 0), (0, 0)]
    padded = jnp.pad(blocks, widths)
    return jnp.stack([lax.slice_in_dim(padded, offsets - 1 - offset, offsets - 1 - offset + block_count, axis=leading + 1)
                      for offset in range(offsets)])


def reference(greens, moment_rate, bin_owner, bin_local):
    toeplitz = kernel_table(moment_rate).astype(jnp.float32)
    bin_index = (bin_owner[:, :, 0] * BIN_DEV + bin_local).astype(jnp.int32)

    def one_site(chosen):
        gathered = greens[chosen].astype(jnp.float32)
        shifted = stack_blocks(gathered, toeplitz.shape[0])
        summed = jnp.einsum('ocnsj,osjy->cny', shifted, toeplitz)
        return summed.reshape(CH, NT // TB, VAR, TB).transpose(2, 0, 1, 3).reshape(VAR, CH, NT).astype(jnp.bfloat16)

    return lax.map(one_site, bin_index)
```

```python
import functools
import jax
import jax.numpy as jnp
from jax import lax
from jax.experimental import pallas as pl
from jax.experimental.pallas import tpu as pltpu
from jax.sharding import PartitionSpec as P

MESH = pl.DeviceIdType.MESH
NX, NZ = 4, 8
NXZ = NX * NZ
CAP = 3
HALF = 64
LANES = 128
LEVELS = 2


def plan():
    jobs = [s * k for k in range(LEVELS, 0, -1) for s in (1, -1)] + [0]
    groups = {job: [] for job in jobs}
    for dz in (4, 3, -3, 2, -2, 1, -1, 0):
        for dx in (2, 1, 3, 0):
            sign = (1 if dx in (0, 1) else -1) if dz == 4 else (1 if dz > 0 else -1)
            far = sign * abs(dz)
            hop = sign * max(abs(dz) - LEVELS, 0)
            groups[far - hop].append((dx, dz, hop))
    order, spans = [], {}
    for job in jobs:
        spans[job] = (len(order), len(order) + len(groups[job]))
        order += groups[job]
    sends = []
    for k in range(LEVELS, 0, -1):
        for pair in zip(groups[k], groups[-k]):
            sends += pair
    sends += groups[0]
    return jobs, order, spans, [order.index(g) for g in sends]


def kernel(
    greens, moment, owner, local_bin, out,
    rows, land, sent, toep, base, moments, moment_out, table_out, tables, table_smem,
    left, acc, inbox,
    rows_sem, smem_sem, table_send, table_recv, moment_send, moment_recv, row_send, row_recv, sum_send, sum_recv,
):
    jobs, order, spans, send_order = plan()
    bins = lax.axis_index("bins")
    site = lax.axis_index("sites")
    x, z = site // NZ, site % NZ
    nbins = moments.shape[0]

    def at(px, pz):
        return (px + NX) % NX * NZ + (pz + NZ) % NZ

    def table_copy(step):
        other = (site + step) % NXZ
        return pltpu.make_async_remote_copy(
            table_out, tables.at[site], table_send.at[step - 1], table_recv.at[step - 1],
            device_id=(bins, other), device_id_type=MESH,
        )

    def moment_copy(step):
        other = (bins + step) % nbins
        return pltpu.make_async_remote_copy(
            moment_out, moments.at[bins], moment_send.at[step - 1], moment_recv.at[step - 1],
            device_id=(other, site), device_id_type=MESH,
        )

    def row_copy(g):
        dx, dz, hop = order[g]
        return pltpu.make_async_remote_copy(
            sent.at[pl.ds(CAP * g, CAP)], land.at[pl.ds(CAP * g, CAP)], row_send.at[g], row_recv.at[g],
            device_id=(bins, at(x + dx, z + hop)), device_id_type=MESH,
        )

    def box(job):
        return 0 if job > 0 else 1, abs(job) - 1

    def sum_copy(job, p):
        side, level = box(job)
        index = (side * LEVELS + level) * 4 + p
        return pltpu.make_async_remote_copy(
            acc.at[jobs.index(job), p], inbox.at[side, level, p], sum_send.at[index], sum_recv.at[index],
            device_id=(bins, at(x, z + (1 if job > 0 else -1))), device_id_type=MESH,
        )

    fetch = pltpu.make_async_copy(greens, rows, rows_sem)
    fetch.start()

    barrier = pltpu.get_barrier_semaphore()

    @pl.loop(1, NXZ)
    def _(step):
        pl.semaphore_signal(barrier, inc=1, device_id=(bins, (site + step) % NXZ), device_id_type=MESH)

    @pl.loop(1, nbins)
    def _(step):
        pl.semaphore_signal(barrier, inc=1, device_id=((bins + step) % nbins, site), device_id_type=MESH)

    faults = owner.shape[1]
    fault = lax.broadcasted_iota(jnp.int32, (faults, LANES), 0)
    hit = owner[0] == lax.broadcasted_iota(jnp.int32, (faults, LANES), 1)
    rank = hit.astype(jnp.int32)
    shift = 1
    while shift < faults:
        rank += jnp.concatenate([jnp.zeros((shift, LANES), jnp.int32), rank[:-shift]], axis=0)
        shift *= 2
    square = (faults, faults)
    diagonal = lax.broadcasted_iota(jnp.int32, square, 0) == lax.broadcasted_iota(jnp.int32, square, 1)
    wanted = jnp.sum(jnp.where(diagonal, local_bin[...] + 1, 0), axis=1, keepdims=True)
    lines = []
    for r in range(CAP):
        here = hit & (rank == r + 1)
        lines.append(jnp.sum(jnp.where(here, wanted, 0), axis=0, keepdims=True))
        lines.append(jnp.sum(jnp.where(here, fault + 1, 0), axis=0, keepdims=True))
    table = jnp.concatenate(lines + [jnp.zeros((8 - 2 * CAP, LANES), jnp.int32)], axis=0)
    table_out[...] = table
    tables[site] = table
    own_rate = jnp.concatenate([moment[0], jnp.zeros((faults, HALF), jnp.bfloat16)], axis=1)
    moment_out[...] = own_rate
    moments[bins] = own_rate

    pl.semaphore_wait(barrier, NXZ - 1 + nbins - 1)

    @pl.loop(1, NXZ)
    def _(step):
        table_copy(step).start()

    @pl.loop(1, nbins)
    def _(step):
        moment_copy(step).start()

    acc[...] = jnp.zeros_like(acc)

    @pl.loop(1, NXZ)
    def _(step):
        table_copy(step).wait_recv()

    to_smem = pltpu.make_async_copy(tables, table_smem, smem_sem)
    to_smem.start()
    to_smem.wait()
    fetch.wait()

    for g in send_order:
        dx, dz, hop = order[g]
        here = dx == 0 and hop == 0
        asking = at(x + dx, z + dz)
        target = land if here else sent

        def gather(r, _, g=g, asking=asking, target=target):
            row = rows[jnp.maximum(table_smem[asking, 2 * r, site] - 1, 0)]
            target[CAP * g + r] = jnp.concatenate(
                [row[:, LANES * m : LANES * (m + 1)] for m in range(row.shape[1] // LANES)], axis=0
            )
            return 0

        lax.fori_loop(0, CAP, gather, 0)
        if not here:
            row_copy(g).start()

    for g, (dx, dz, hop) in enumerate(order):
        asking = at(x, z - hop + dz)
        source = at(x - dx, z - hop)
        for r in range(CAP):
            left[CAP * g + r] = table_smem[asking, 2 * r + 1, source]

    @pl.loop(1, nbins)
    def _(step):
        moment_copy(step).wait_recv()

    for p in range(4):
        base[p] = moments[2 * p + 1].astype(jnp.float32) + pltpu.roll(
            moments[2 * p].astype(jnp.float32), HALF, 1
        )
    lane = lax.broadcasted_iota(jnp.int32, (LANES, LANES), 1)
    lag = lane - lax.broadcasted_iota(jnp.int32, (LANES, LANES), 0)
    inside = ((lane < HALF) & (lag < 0) & (lag >= -HALF)) | ((lane >= HALF) & (lag >= 0) & (lag < HALF))
    toep[0] = jnp.zeros(toep.shape[1:], toep.dtype)

    @pl.loop(0, faults)
    def _(f):
        for p in range(4):
            spread = jnp.broadcast_to(base[p, pl.ds(f, 1), :], (LANES, LANES))
            turned = pltpu.roll(spread, 0, 1, stride=1, stride_axis=0)
            toep[f + 1, :, LANES * p : LANES * (p + 1)] = jnp.where(inside, turned, 0.0).astype(jnp.bfloat16)

    def window(slot):
        now = land[slot]
        swapped = pltpu.roll(now.astype(jnp.float32), HALF, 1)
        before = jnp.concatenate([jnp.zeros((8, LANES), jnp.float32), swapped[:-8]], axis=0)
        early = jnp.where(lane < HALF, before, swapped)
        return jnp.concatenate([early.astype(jnp.bfloat16), now], axis=0)

    def add_groups(job):
        first, last = spans[job]
        for g in range(first, last):
            dx, dz, hop = order[g]
            if dx != 0 or hop != 0:
                row_copy(g).wait_recv()

        def pair(i, _):
            slot = CAP * first + 2 * i
            a = jnp.concatenate([window(slot), window(slot + 1)], axis=1)
            b = jnp.concatenate([toep[left[slot]], toep[left[slot + 1]]], axis=0)
            c = jnp.dot(a, b, preferred_element_type=jnp.float32)
            for p in range(4):
                acc[jobs.index(job), p] += c[:, LANES * p : LANES * (p + 1)]
            return 0

        lax.fori_loop(0, CAP * (last - first) // 2, pair, 0)

    for job in jobs:
        add_groups(job)
        if job == 0:
            continue
        for p in range(4):
            if abs(job) < LEVELS:
                further = job + (1 if job > 0 else -1)
                sum_copy(further, p).wait_recv()
                side, level = box(further)
                acc[jobs.index(job), p] += inbox[side, level, p]
            sum_copy(job, p).start()

    half = lax.broadcasted_iota(jnp.int32, (8, LANES), 1) < HALF
    for p in range(4):
        total = acc[jobs.index(0), p]
        if LEVELS > 0:
            for job in (1, -1):
                sum_copy(job, p).wait_recv()
                side, level = box(job)
                total = total + inbox[side, level, p]
        for m in range(LANES // 8):
            early = total[8 * m : 8 * m + 8]
            late = total[LANES + 8 * m : LANES + 8 * m + 8]
            where = slice(LANES * m, LANES * (m + 1))
            out[0, 2 * p, :, where] = jnp.where(half, early, pltpu.roll(late, HALF, 1)).astype(out.dtype)
            out[0, 2 * p + 1, :, where] = jnp.where(half, pltpu.roll(early, HALF, 1), late).astype(out.dtype)

    @pl.loop(1, NXZ)
    def _(step):
        table_copy(step).wait_send()

    @pl.loop(1, nbins)
    def _(step):
        moment_copy(step).wait_send()

    for g, (dx, dz, hop) in enumerate(order):
        if dx != 0 or hop != 0:
            row_copy(g).wait_send()
    for job in jobs:
        if job != 0:
            for p in range(4):
                sum_copy(job, p).wait_send()


def local(greens, moment_rate, bin_owner, bin_local):
    bins, channels, samples = greens.shape
    nbins = lax.axis_size("bins")
    faults = moment_rate.shape[1]
    slots = NXZ * CAP
    vmem, dma = pltpu.VMEM, pltpu.SemaphoreType.DMA
    sums = 2 * LEVELS + 1
    return pl.pallas_call(
        kernel,
        out_shape=jax.ShapeDtypeStruct((1, nbins, channels, samples), jnp.bfloat16),
        in_specs=[
            pl.BlockSpec(memory_space=pl.ANY),
            pl.BlockSpec(memory_space=vmem),
            pl.BlockSpec(memory_space=vmem),
            pl.BlockSpec(memory_space=vmem),
        ],
        out_specs=pl.BlockSpec(memory_space=vmem),
        scratch_shapes=[
            vmem((bins, channels, samples), jnp.bfloat16),
            vmem((slots, LANES, LANES), jnp.bfloat16),
            vmem((slots, LANES, LANES), jnp.bfloat16),
            vmem((faults + 1, LANES, 4 * LANES), jnp.bfloat16),
            vmem((4, faults, LANES), jnp.float32),
            vmem((nbins, faults, LANES), jnp.bfloat16),
            vmem((faults, LANES), jnp.bfloat16),
            vmem((8, LANES), jnp.int32),
            vmem((NXZ, 8, LANES), jnp.int32),
            pltpu.SMEM((NXZ, 8, LANES), jnp.int32),
            pltpu.SMEM((slots,), jnp.int32),
            vmem((sums, 4, 2 * LANES, LANES), jnp.float32),
            vmem((2, max(LEVELS, 1), 4, 2 * LANES, LANES), jnp.float32),
            dma,
            dma,
            dma((NXZ - 1,)),
            dma((NXZ - 1,)),
            dma((nbins - 1,)),
            dma((nbins - 1,)),
            dma((NXZ,)),
            dma((NXZ,)),
            dma((8 * max(LEVELS, 1),)),
            dma((8 * max(LEVELS, 1),)),
        ],
        compiler_params=pltpu.CompilerParams(
            collective_id=0, has_side_effects=True, vmem_limit_bytes=48 * 2**20
        ),
        cost_estimate=pl.CostEstimate(
            flops=slots * 2 * 256 * 128 * 512, bytes_accessed=2 * greens.size, transcendentals=0
        ),
    )(greens, moment_rate, bin_owner, bin_local)


def solution(mesh):
    placed = (
        P("sites", None, None),
        P("bins", None, None),
        P(("bins", "sites"), None, None),
        P(("bins", "sites"), None),
    )
    return jax.shard_map(
        local,
        mesh=mesh,
        in_specs=placed,
        out_specs=P(("bins", "sites"), None, None, None),
        check_vma=False,
    )
```

```python
import functools
import jax
import jax.numpy as jnp
from jax import lax
from jax.experimental import pallas as pl
from jax.experimental.pallas import tpu as pltpu
from jax.sharding import PartitionSpec as P

MESH = pl.DeviceIdType.MESH
NX, NZ = 4, 8
NXZ = NX * NZ
CAP = 3
HALF = 64
LANES = 128
LEVELS = 2
PARTS = 2


def plan():
    jobs = [s * k for k in range(LEVELS, 0, -1) for s in (1, -1)] + [0]
    groups = {job: [] for job in jobs}
    for dz in (4, 3, -3, 2, -2, 1, -1, 0):
        for dx in (2, 1, 3, 0):
            sign = (1 if dx in (0, 1) else -1) if dz == 4 else (1 if dz > 0 else -1)
            far = sign * abs(dz)
            hop = sign * max(abs(dz) - LEVELS, 0)
            groups[far - hop].append((dx, dz, hop))
    order, spans = [], {}
    for job in jobs:
        spans[job] = (len(order), len(order) + len(groups[job]))
        order += groups[job]
    ordered = []
    for k in range(LEVELS, 0, -1):
        ordered.append([g for pair in zip(groups[k], groups[-k]) for g in pair])
    ordered.append(groups[0])
    sends = []
    for h in range(PARTS):
        sends += [(h, order.index(g)) for level in ordered[:-1] for g in level]
    for h in range(PARTS):
        sends += [(h, order.index(g)) for g in ordered[-1]]
    return jobs, order, spans, sends


def kernel(
    greens_hbm, moment_hbm, owner_hbm, bin_hbm, out,
    moment, owner, local_bin, rows, land, sent, toep, base, moments, moment_out, table_out, tables, table_smem,
    left, windows, acc, inbox,
    fetch_sem, smem_sem, table_sem, moment_sem, row_send, row_recv, sum_send, sum_recv,
):
    jobs, order, spans, sends = plan()
    bins = lax.axis_index("bins")
    site = lax.axis_index("sites")
    x, z = site // NZ, site % NZ
    nbins = moments.shape[0]
    part = land.shape[2]

    def at(px, pz):
        return (px + NX) % NX * NZ + (pz + NZ) % NZ

    def table_copy(step):
        return pltpu.make_async_remote_copy(
            table_out, tables.at[site], table_sem.at[0], table_sem.at[1],
            device_id=(bins, (site + step) % NXZ), device_id_type=MESH,
        )

    def moment_copy(step):
        return pltpu.make_async_remote_copy(
            moment_out, moments.at[bins], moment_sem.at[0], moment_sem.at[1],
            device_id=((bins + step) % nbins, site), device_id_type=MESH,
        )

    def all_tables(sem):
        some = tables.at[pl.ds(0, NXZ - 1)]
        return pltpu.make_async_copy(some, some, sem)

    def all_moments(sem):
        some = moments.at[pl.ds(0, nbins - 1)]
        return pltpu.make_async_copy(some, some, sem)

    def row_copy(h, g):
        dx, dz, hop = order[g]
        return pltpu.make_async_remote_copy(
            sent.at[h, pl.ds(CAP * g, CAP)], land.at[h, pl.ds(CAP * g, CAP)], row_send.at[h, g], row_recv.at[h, g],
            device_id=(bins, at(x + dx, z + hop)), device_id_type=MESH,
        )

    def stays(g):
        return order[g][0] == 0 and order[g][2] == 0

    def box(job):
        return 0 if job > 0 else 1, abs(job) - 1

    def sum_copy(h, job, p):
        side, level = box(job)
        index = ((h * 2 + side) * LEVELS + level) * 4 + p
        return pltpu.make_async_remote_copy(
            acc.at[h, jobs.index(job), p], inbox.at[h, side, level, p], sum_send.at[index], sum_recv.at[index],
            device_id=(bins, at(x, z + (1 if job > 0 else -1))), device_id_type=MESH,
        )

    barrier = pltpu.get_barrier_semaphore()
    for step in range(1, NXZ):
        pl.semaphore_signal(barrier, inc=1, device_id=(bins, (site + step) % NXZ), device_id_type=MESH)
    for step in range(1, nbins):
        pl.semaphore_signal(barrier, inc=1, device_id=((bins + step) % nbins, site), device_id_type=MESH)

    fetches = [
        pltpu.make_async_copy(there, here, fetch_sem.at[i])
        for i, (there, here) in enumerate(
            ((owner_hbm, owner), (bin_hbm, local_bin), (moment_hbm, moment), (greens_hbm, rows))
        )
    ]
    for fetch in fetches:
        fetch.start()

    for fetch in fetches[:3]:
        fetch.wait()
    faults = owner.shape[1]
    fault = lax.broadcasted_iota(jnp.int32, (faults, LANES), 0)
    spot = lax.broadcasted_iota(jnp.int32, (faults, LANES), 1)
    square = (faults, faults)
    diagonal = lax.broadcasted_iota(jnp.int32, square, 0) == lax.broadcasted_iota(jnp.int32, square, 1)
    serving = jnp.sum(jnp.where(diagonal, owner[...], 0), axis=1, keepdims=True)
    wanted = jnp.sum(jnp.where(diagonal, local_bin[...] + 1, 0), axis=1, keepdims=True)
    hit = serving == spot % NXZ
    rank = hit.astype(jnp.int32)
    shift = 1
    while shift < faults:
        rank += jnp.concatenate([jnp.zeros((shift, LANES), jnp.int32), rank[:-shift]], axis=0)
        shift *= 2
    chosen = hit & (rank == spot // NXZ + 1)
    table = jnp.sum(jnp.where(chosen, wanted * 65536 + fault + 1, 0), axis=0, keepdims=True)
    table_out[...] = table
    tables[site] = table
    own_rate = jnp.concatenate([moment[0], jnp.zeros((faults, HALF), jnp.bfloat16)], axis=1)
    moment_out[...] = own_rate
    moments[bins] = own_rate

    pl.semaphore_wait(barrier, NXZ - 1 + nbins - 1)
    for step in range(1, NXZ):
        table_copy(step).start()
    all_tables(table_sem.at[1]).wait()
    to_smem = pltpu.make_async_copy(tables, table_smem, smem_sem)
    to_smem.start()
    to_smem.wait()
    fetches[3].wait()

    def pass_on(h, g):
        dx, dz, hop = order[g]
        asking = at(x + dx, z + dz)
        target = land if stays(g) else sent
        samples = part // 8 * LANES

        def gather(r, _):
            row = rows[jnp.maximum(table_smem[asking, 0, NXZ * r + site] // 65536 - 1, 0)]
            row = row[:, samples * h : samples * (h + 1)]
            target[h, CAP * g + r] = jnp.concatenate(
                [row[:, LANES * m : LANES * (m + 1)] for m in range(part // 8)], axis=0
            )
            return 0

        lax.fori_loop(0, CAP, gather, 0)
        if not stays(g):
            row_copy(h, g).start()

    for i, (h, g) in enumerate(sends):
        pass_on(h, g)
        if i == 8:
            for step in range(1, nbins):
                moment_copy(step).start()

    for g, (dx, dz, hop) in enumerate(order):
        asking = at(x, z - hop + dz)
        source = at(x - dx, z - hop)
        for r in range(CAP):
            left[CAP * g + r] = table_smem[asking, 0, NXZ * r + source] % 65536

    all_moments(moment_sem.at[1]).wait()
    for p in range(4):
        base[p] = moments[2 * p + 1].astype(jnp.float32) + pltpu.roll(
            moments[2 * p].astype(jnp.float32), HALF, 1
        )
    square = (LANES, LANES)
    lane = lax.broadcasted_iota(jnp.int32, square, 1)
    lag = lane - lax.broadcasted_iota(jnp.int32, square, 0)
    inside = ((lane < HALF) & (lag < 0) & (lag >= -HALF)) | ((lane >= HALF) & (lag >= 0) & (lag < HALF))
    toep[0] = jnp.zeros(toep.shape[1:], toep.dtype)

    @pl.loop(0, faults)
    def _(f):
        for p in range(4):
            spread = jnp.broadcast_to(base[p, pl.ds(f, 1), :], square)
            turned = pltpu.roll(spread, 0, 1, stride=1, stride_axis=0)
            toep[f + 1, :, LANES * p : LANES * (p + 1)] = jnp.where(inside, turned, 0.0).astype(jnp.bfloat16)

    early_lane = lax.broadcasted_iota(jnp.int32, (part, LANES), 1) < HALF

    def window(h, slot):
        now = land[h, slot]
        swapped = pltpu.roll(now.astype(jnp.float32), HALF, 1)
        if h == 0:
            edge = jnp.zeros((8, LANES), jnp.float32)
        else:
            edge = pltpu.roll(land[h - 1, slot].astype(jnp.float32)[part - 8 :], HALF, 1)
        before = jnp.concatenate([edge, swapped[: part - 8]], axis=0)
        return jnp.concatenate([jnp.where(early_lane, before, swapped).astype(jnp.bfloat16), now], axis=0)

    def own_sums(h, job):
        first, last = spans[job]
        size = min(last - first, 5)
        for start in range(first, last, size):
            for g in range(start, start + size):
                if not stays(g):
                    row_copy(h, g).wait_recv()
            slots = range(CAP * start, CAP * (start + size))
            for i, slot in enumerate(slots):
                windows[:, LANES * i : LANES * (i + 1)] = window(h, slot)
            tiles = jnp.concatenate([toep[left[slot]] for slot in slots], axis=0)
            c = jnp.dot(windows[:, : LANES * len(slots)], tiles, preferred_element_type=jnp.float32)
            for p in range(4):
                mine = c[:, LANES * p : LANES * (p + 1)]
                if start == first:
                    acc[h, jobs.index(job), p] = mine
                else:
                    acc[h, jobs.index(job), p] += mine

    def send_sums(h, job):
        for p in range(4):
            if abs(job) < LEVELS:
                further = job + (1 if job > 0 else -1)
                sum_copy(h, further, p).wait_recv()
                side, level = box(further)
                acc[h, jobs.index(job), p] += inbox[h, side, level, p]
            sum_copy(h, job, p).start()

    half = lax.broadcasted_iota(jnp.int32, (8, LANES), 1) < HALF

    def finish(h):
        for p in range(4):
            total = acc[h, jobs.index(0), p]
            for job in (1, -1):
                sum_copy(h, job, p).wait_recv()
                side, level = box(job)
                total = total + inbox[h, side, level, p]
            for m in range(part // 8):
                early = total[8 * m : 8 * m + 8]
                late = total[part + 8 * m : part + 8 * m + 8]
                start = part // 8 * LANES * h + LANES * m
                where = slice(start, start + LANES)
                out[0, 2 * p, :, where] = jnp.where(half, early, pltpu.roll(late, HALF, 1)).astype(out.dtype)
                out[0, 2 * p + 1, :, where] = jnp.where(half, pltpu.roll(early, HALF, 1), late).astype(out.dtype)

    for h in range(PARTS):
        for k in range(LEVELS, 0, -1):
            if k == 1 and h > 0:
                own_sums(h - 1, 0)
            for job in (k, -k):
                own_sums(h, job)
                if k == LEVELS:
                    send_sums(h, job)
            if k < LEVELS:
                for job in (k, -k):
                    send_sums(h, job)
    own_sums(PARTS - 1, 0)
    for h in range(PARTS):
        finish(h)

    all_tables(table_sem.at[0]).wait()
    all_moments(moment_sem.at[0]).wait()
    for h in range(PARTS):
        for g in range(len(order)):
            if not stays(g):
                row_copy(h, g).wait_send()
        for job in jobs:
            if job != 0:
                for p in range(4):
                    sum_copy(h, job, p).wait_send()


def local(greens, moment_rate, bin_owner, bin_local):
    bins, channels, samples = greens.shape
    nbins = lax.axis_size("bins")
    faults = moment_rate.shape[1]
    slots = NXZ * CAP
    part = samples // LANES * channels // PARTS
    vmem, dma = pltpu.VMEM, pltpu.SemaphoreType.DMA
    sums = 2 * LEVELS + 1
    return pl.pallas_call(
        kernel,
        out_shape=jax.ShapeDtypeStruct((1, nbins, channels, samples), jnp.bfloat16),
        in_specs=[pl.BlockSpec(memory_space=pltpu.HBM)] * 4,
        out_specs=pl.BlockSpec(memory_space=vmem),
        scratch_shapes=[
            vmem(moment_rate.shape, jnp.bfloat16),
            vmem(bin_local.shape, jnp.int32),
            vmem(bin_local.shape, jnp.int32),
            vmem((bins, channels, samples), jnp.bfloat16),
            vmem((PARTS, slots, part, LANES), jnp.bfloat16),
            vmem((PARTS, slots, part, LANES), jnp.bfloat16),
            vmem((faults + 1, LANES, 4 * LANES), jnp.bfloat16),
            vmem((4, faults, LANES), jnp.float32),
            vmem((nbins, faults, LANES), jnp.bfloat16),
            vmem((faults, LANES), jnp.bfloat16),
            vmem((1, LANES), jnp.int32),
            vmem((NXZ, 1, LANES), jnp.int32),
            pltpu.SMEM((NXZ, 1, LANES), jnp.int32),
            pltpu.SMEM((slots,), jnp.int32),
            vmem((2 * part, 5 * CAP * LANES), jnp.bfloat16),
            vmem((PARTS, sums, 4, 2 * part, LANES), jnp.float32),
            vmem((PARTS, 2, LEVELS, 4, 2 * part, LANES), jnp.float32),
            dma((4,)),
            dma,
            dma((2,)),
            dma((2,)),
            dma((PARTS, NXZ)),
            dma((PARTS, NXZ)),
            dma((PARTS * LEVELS * 8,)),
            dma((PARTS * LEVELS * 8,)),
        ],
        compiler_params=pltpu.CompilerParams(
            collective_id=0, has_side_effects=True, vmem_limit_bytes=64 * 2**20
        ),
        cost_estimate=pl.CostEstimate(
            flops=slots * 2 * 256 * 128 * 512, bytes_accessed=2 * greens.size, transcendentals=0
        ),
    )(greens, moment_rate, bin_owner.reshape(bin_local.shape), bin_local)


def solution(mesh):
    placed = (
        P("sites", None, None),
        P("bins", None, None),
        P(("bins", "sites"), None, None),
        P(("bins", "sites"), None),
    )
    return jax.shard_map(
        local,
        mesh=mesh,
        in_specs=placed,
        out_specs=P(("bins", "sites"), None, None, None),
        check_vma=False,
    )
```

```python
import functools
import jax
import jax.numpy as jnp
from jax import lax
from jax.experimental import pallas as pl
from jax.experimental.pallas import tpu as pltpu
from jax.sharding import PartitionSpec as P

MESH = pl.DeviceIdType.MESH
NX, NZ = 4, 8
NXZ = NX * NZ
CAP = 3
HALF = 64
LANES = 128
LEVELS = 2
PARTS = 2


def plan():
    jobs = [s * k for k in range(LEVELS, 0, -1) for s in (1, -1)] + [0]
    groups = {job: [] for job in jobs}
    for dz in (2, -2, 3, -3, 4, 1, -1, 0):
        for dx in (1, 2, 3, 0):
            sign = (1 if dx in (0, 1) else -1) if dz == 4 else (1 if dz > 0 else -1)
            far = sign * abs(dz)
            hop = sign * max(abs(dz) - LEVELS, 0)
            groups[far - hop].append((dx, dz, hop))
    order, spans = [], {}
    for job in jobs:
        spans[job] = (len(order), len(order) + len(groups[job]))
        order += groups[job]
    ordered = []
    for k in range(LEVELS, 0, -1):
        ordered.append([g for pair in zip(groups[k], groups[-k]) for g in pair])
    ordered.append(groups[0])
    sends = []
    for h in range(PARTS):
        sends += [(h, order.index(g)) for level in ordered[:-1] for g in level]
    for h in range(PARTS):
        sends += [(h, order.index(g)) for g in ordered[-1]]
    return jobs, order, spans, sends


def kernel(
    greens_hbm, moment_hbm, owner_hbm, bin_hbm, out,
    moment, owner, local_bin, rows, land, sent, toep, base, moments, moment_out, table_out, tables, table_smem,
    left, windows, acc, inbox,
    fetch_sem, smem_sem, table_sem, moment_sem, row_send, row_recv, sum_send, sum_recv,
):
    jobs, order, spans, sends = plan()
    bins = lax.axis_index("bins")
    site = lax.axis_index("sites")
    x, z = site // NZ, site % NZ
    nbins = moments.shape[0]
    part = land.shape[2]

    def at(px, pz):
        return (px + NX) % NX * NZ + (pz + NZ) % NZ

    def table_copy(step):
        return pltpu.make_async_remote_copy(
            table_out, tables.at[site], table_sem.at[0], table_sem.at[1],
            device_id=(bins, (site + step) % NXZ), device_id_type=MESH,
        )

    def moment_copy(step):
        return pltpu.make_async_remote_copy(
            moment_out, moments.at[bins], moment_sem.at[0], moment_sem.at[1],
            device_id=((bins + step) % nbins, site), device_id_type=MESH,
        )

    def all_tables(sem):
        some = tables.at[pl.ds(0, NXZ - 1)]
        return pltpu.make_async_copy(some, some, sem)

    def all_moments(sem):
        some = moments.at[pl.ds(0, nbins - 1)]
        return pltpu.make_async_copy(some, some, sem)

    def row_copy(h, g):
        dx, dz, hop = order[g]
        return pltpu.make_async_remote_copy(
            sent.at[h, pl.ds(CAP * g, CAP)], land.at[h, pl.ds(CAP * g, CAP)], row_send.at[h, g], row_recv.at[h, g],
            device_id=(bins, at(x + dx, z + hop)), device_id_type=MESH,
        )

    def stays(g):
        return order[g][0] == 0 and order[g][2] == 0

    def box(job):
        return 0 if job > 0 else 1, abs(job) - 1

    def sum_copy(h, job, p):
        side, level = box(job)
        index = ((h * 2 + side) * LEVELS + level) * 4 + p
        return pltpu.make_async_remote_copy(
            acc.at[h, jobs.index(job), p], inbox.at[h, side, level, p], sum_send.at[index], sum_recv.at[index],
            device_id=(bins, at(x, z + (1 if job > 0 else -1))), device_id_type=MESH,
        )

    barrier = pltpu.get_barrier_semaphore()
    for step in range(1, NXZ):
        pl.semaphore_signal(barrier, inc=1, device_id=(bins, (site + step) % NXZ), device_id_type=MESH)
    for step in range(1, nbins):
        pl.semaphore_signal(barrier, inc=1, device_id=((bins + step) % nbins, site), device_id_type=MESH)

    fetches = [
        pltpu.make_async_copy(there, here, fetch_sem.at[i])
        for i, (there, here) in enumerate(
            ((owner_hbm, owner), (bin_hbm, local_bin), (moment_hbm, moment), (greens_hbm, rows))
        )
    ]
    for fetch in fetches:
        fetch.start()

    for fetch in fetches[:3]:
        fetch.wait()
    faults = owner.shape[1]
    fault = lax.broadcasted_iota(jnp.int32, (faults, LANES), 0)
    spot = lax.broadcasted_iota(jnp.int32, (faults, LANES), 1)
    square = (faults, faults)
    diagonal = lax.broadcasted_iota(jnp.int32, square, 0) == lax.broadcasted_iota(jnp.int32, square, 1)
    serving = jnp.sum(jnp.where(diagonal, owner[...], 0), axis=1, keepdims=True)
    wanted = jnp.sum(jnp.where(diagonal, local_bin[...] + 1, 0), axis=1, keepdims=True)
    hit = serving == spot % NXZ
    rank = hit.astype(jnp.int32)
    shift = 1
    while shift < faults:
        rank += jnp.concatenate([jnp.zeros((shift, LANES), jnp.int32), rank[:-shift]], axis=0)
        shift *= 2
    chosen = hit & (rank == spot // NXZ + 1)
    table = jnp.sum(jnp.where(chosen, wanted * 65536 + fault + 1, 0), axis=0, keepdims=True)
    table_out[...] = table
    tables[site] = table
    own_rate = jnp.concatenate([moment[0], jnp.zeros((faults, HALF), jnp.bfloat16)], axis=1)
    moment_out[...] = own_rate
    moments[bins] = own_rate

    pl.semaphore_wait(barrier, NXZ - 1 + nbins - 1)
    for step in range(1, NXZ):
        table_copy(step).start()
    all_tables(table_sem.at[1]).wait()
    to_smem = pltpu.make_async_copy(tables, table_smem, smem_sem)
    to_smem.start()
    to_smem.wait()
    fetches[3].wait()

    def pass_on(h, g):
        dx, dz, hop = order[g]
        asking = at(x + dx, z + dz)
        target = land if stays(g) else sent
        samples = part // 8 * LANES

        def gather(r, _):
            row = rows[jnp.maximum(table_smem[asking, 0, NXZ * r + site] // 65536 - 1, 0)]
            row = row[:, samples * h : samples * (h + 1)]
            target[h, CAP * g + r] = jnp.concatenate(
                [row[:, LANES * m : LANES * (m + 1)] for m in range(part // 8)], axis=0
            )
            return 0

        lax.fori_loop(0, CAP, gather, 0)
        if not stays(g):
            row_copy(h, g).start()

    for i, (h, g) in enumerate(sends):
        pass_on(h, g)
        if i == 8:
            for step in range(1, nbins):
                moment_copy(step).start()

    for g, (dx, dz, hop) in enumerate(order):
        asking = at(x, z - hop + dz)
        source = at(x - dx, z - hop)
        for r in range(CAP):
            left[CAP * g + r] = table_smem[asking, 0, NXZ * r + source] % 65536

    all_moments(moment_sem.at[1]).wait()
    for p in range(4):
        base[p] = moments[2 * p + 1].astype(jnp.float32) + pltpu.roll(
            moments[2 * p].astype(jnp.float32), HALF, 1
        )
    square = (LANES, LANES)
    lane = lax.broadcasted_iota(jnp.int32, square, 1)
    lag = lane - lax.broadcasted_iota(jnp.int32, square, 0)
    inside = ((lane < HALF) & (lag < 0) & (lag >= -HALF)) | ((lane >= HALF) & (lag >= 0) & (lag < HALF))
    toep[0] = jnp.zeros(toep.shape[1:], toep.dtype)

    @pl.loop(0, faults)
    def _(f):
        for p in range(4):
            spread = jnp.broadcast_to(base[p, pl.ds(f, 1), :], square)
            turned = pltpu.roll(spread, 0, 1, stride=1, stride_axis=0)
            toep[f + 1, :, LANES * p : LANES * (p + 1)] = jnp.where(inside, turned, 0.0).astype(jnp.bfloat16)

    early_lane = lax.broadcasted_iota(jnp.int32, (part, LANES), 1) < HALF

    def window(h, slot):
        now = land[h, slot]
        swapped = pltpu.roll(now.astype(jnp.float32), HALF, 1)
        if h == 0:
            edge = jnp.zeros((8, LANES), jnp.float32)
        else:
            edge = pltpu.roll(land[h - 1, slot].astype(jnp.float32)[part - 8 :], HALF, 1)
        before = jnp.concatenate([edge, swapped[: part - 8]], axis=0)
        return jnp.concatenate([jnp.where(early_lane, before, swapped).astype(jnp.bfloat16), now], axis=0)

    def own_sums(h, job):
        first, last = spans[job]
        size = min(last - first, 5)
        for start in range(first, last, size):
            for g in range(start, start + size):
                if not stays(g):
                    row_copy(h, g).wait_recv()
            slots = range(CAP * start, CAP * (start + size))
            for i, slot in enumerate(slots):
                windows[:, LANES * i : LANES * (i + 1)] = window(h, slot)
            tiles = jnp.concatenate([toep[left[slot]] for slot in slots], axis=0)
            c = jnp.dot(windows[:, : LANES * len(slots)], tiles, preferred_element_type=jnp.float32)
            for p in range(4):
                mine = c[:, LANES * p : LANES * (p + 1)]
                if start == first:
                    acc[h, jobs.index(job), p] = mine
                else:
                    acc[h, jobs.index(job), p] += mine

    def send_sums(h, job):
        for p in range(4):
            if abs(job) < LEVELS:
                further = job + (1 if job > 0 else -1)
                sum_copy(h, further, p).wait_recv()
                side, level = box(further)
                acc[h, jobs.index(job), p] += inbox[h, side, level, p]
            sum_copy(h, job, p).start()

    half = lax.broadcasted_iota(jnp.int32, (8, LANES), 1) < HALF

    def finish(h):
        for p in range(4):
            total = acc[h, jobs.index(0), p]
            for job in (1, -1):
                sum_copy(h, job, p).wait_recv()
                side, level = box(job)
                total = total + inbox[h, side, level, p]
            for m in range(part // 8):
                early = total[8 * m : 8 * m + 8]
                late = total[part + 8 * m : part + 8 * m + 8]
                start = part // 8 * LANES * h + LANES * m
                where = slice(start, start + LANES)
                out[0, 2 * p, :, where] = jnp.where(half, early, pltpu.roll(late, HALF, 1)).astype(out.dtype)
                out[0, 2 * p + 1, :, where] = jnp.where(half, pltpu.roll(early, HALF, 1), late).astype(out.dtype)

    for h in range(PARTS):
        for k in range(LEVELS, 0, -1):
            if k == 1 and h > 0:
                own_sums(h - 1, 0)
            for job in (k, -k):
                own_sums(h, job)
                if k == LEVELS:
                    send_sums(h, job)
            if k < LEVELS:
                for job in (k, -k):
                    send_sums(h, job)
    own_sums(PARTS - 1, 0)
    for h in range(PARTS):
        finish(h)

    all_tables(table_sem.at[0]).wait()
    all_moments(moment_sem.at[0]).wait()
    for h in range(PARTS):
        for g in range(len(order)):
            if not stays(g):
                row_copy(h, g).wait_send()
        for job in jobs:
            if job != 0:
                for p in range(4):
                    sum_copy(h, job, p).wait_send()


def local(greens, moment_rate, bin_owner, bin_local):
    bins, channels, samples = greens.shape
    nbins = lax.axis_size("bins")
    faults = moment_rate.shape[1]
    slots = NXZ * CAP
    part = samples // LANES * channels // PARTS
    vmem, dma = pltpu.VMEM, pltpu.SemaphoreType.DMA
    sums = 2 * LEVELS + 1
    return pl.pallas_call(
        kernel,
        out_shape=jax.ShapeDtypeStruct((1, nbins, channels, samples), jnp.bfloat16),
        in_specs=[pl.BlockSpec(memory_space=pltpu.HBM)] * 4,
        out_specs=pl.BlockSpec(memory_space=vmem),
        scratch_shapes=[
            vmem(moment_rate.shape, jnp.bfloat16),
            vmem(bin_local.shape, jnp.int32),
            vmem(bin_local.shape, jnp.int32),
            vmem((bins, channels, samples), jnp.bfloat16),
            vmem((PARTS, slots, part, LANES), jnp.bfloat16),
            vmem((PARTS, slots, part, LANES), jnp.bfloat16),
            vmem((faults + 1, LANES, 4 * LANES), jnp.bfloat16),
            vmem((4, faults, LANES), jnp.float32),
            vmem((nbins, faults, LANES), jnp.bfloat16),
            vmem((faults, LANES), jnp.bfloat16),
            vmem((1, LANES), jnp.int32),
            vmem((NXZ, 1, LANES), jnp.int32),
            pltpu.SMEM((NXZ, 1, LANES), jnp.int32),
            pltpu.SMEM((slots,), jnp.int32),
            vmem((2 * part, 5 * CAP * LANES), jnp.bfloat16),
            vmem((PARTS, sums, 4, 2 * part, LANES), jnp.float32),
            vmem((PARTS, 2, LEVELS, 4, 2 * part, LANES), jnp.float32),
            dma((4,)),
            dma,
            dma((2,)),
            dma((2,)),
            dma((PARTS, NXZ)),
            dma((PARTS, NXZ)),
            dma((PARTS * LEVELS * 8,)),
            dma((PARTS * LEVELS * 8,)),
        ],
        compiler_params=pltpu.CompilerParams(
            collective_id=0, has_side_effects=True, vmem_limit_bytes=64 * 2**20
        ),
        cost_estimate=pl.CostEstimate(
            flops=slots * 2 * 256 * 128 * 512, bytes_accessed=2 * greens.size, transcendentals=0
        ),
    )(greens, moment_rate, bin_owner.reshape(bin_local.shape), bin_local)


def solution(mesh):
    placed = (
        P("sites", None, None),
        P("bins", None, None),
        P(("bins", "sites"), None, None),
        P(("bins", "sites"), None),
    )
    return jax.shard_map(
        local,
        mesh=mesh,
        in_specs=placed,
        out_specs=P(("bins", "sites"), None, None, None),
        check_vma=False,
    )
```

```python
import functools
import jax
import jax.numpy as jnp
from jax import lax
from jax.experimental import pallas as pl
from jax.experimental.pallas import tpu as pltpu
from jax.sharding import PartitionSpec as P

MESH = pl.DeviceIdType.MESH
NX, NZ = 4, 8
NXZ = NX * NZ
CAP = 3
HALF = 64
LANES = 128
LEVELS = 2
PARTS = 2


def plan():
    jobs = [s * k for k in range(LEVELS, 0, -1) for s in (1, -1)] + [0]
    groups = {job: [] for job in jobs}
    for dz in (2, -2, 3, -3, 4, 1, -1, 0):
        for dx in (1, 3, 2, 0):
            sign = (1 if dx in (0, 1) else -1) if dz == 4 else (1 if dz > 0 else -1)
            far = sign * abs(dz)
            hop = sign * max(abs(dz) - LEVELS, 0)
            groups[far - hop].append((dx, dz, hop))
    order, spans = [], {}
    for job in jobs:
        spans[job] = (len(order), len(order) + len(groups[job]))
        order += groups[job]
    ordered = []
    for k in range(LEVELS, 0, -1):
        ordered.append([g for pair in zip(groups[k], groups[-k]) for g in pair])
    ordered.append(groups[0])
    sends = []
    for h in range(PARTS):
        sends += [(h, order.index(g)) for level in ordered[:-1] for g in level]
    for h in range(PARTS):
        sends += [(h, order.index(g)) for g in ordered[-1]]
    return jobs, order, spans, sends


def kernel(
    greens_hbm, moment_hbm, owner_hbm, bin_hbm, out,
    moment, owner, local_bin, rows, land, sent, toep, base, moments, moment_out, table_out, tables, table_smem,
    left, windows, acc, inbox,
    fetch_sem, smem_sem, table_sem, moment_sem, row_send, row_recv, sum_send, sum_recv,
):
    jobs, order, spans, sends = plan()
    bins = lax.axis_index("bins")
    site = lax.axis_index("sites")
    x, z = site // NZ, site % NZ
    nbins = moments.shape[0]
    part = land.shape[2]

    def at(px, pz):
        return (px + NX) % NX * NZ + (pz + NZ) % NZ

    def table_copy(step):
        return pltpu.make_async_remote_copy(
            table_out, tables.at[site], table_sem.at[0], table_sem.at[1],
            device_id=(bins, (site + step) % NXZ), device_id_type=MESH,
        )

    def moment_copy(step):
        return pltpu.make_async_remote_copy(
            moment_out, moments.at[bins], moment_sem.at[0], moment_sem.at[1],
            device_id=((bins + step) % nbins, site), device_id_type=MESH,
        )

    def all_tables(sem):
        some = tables.at[pl.ds(0, NXZ - 1)]
        return pltpu.make_async_copy(some, some, sem)

    def all_moments(sem):
        some = moments.at[pl.ds(0, nbins - 1)]
        return pltpu.make_async_copy(some, some, sem)

    def row_copy(h, g):
        dx, dz, hop = order[g]
        return pltpu.make_async_remote_copy(
            sent.at[h, pl.ds(CAP * g, CAP)], land.at[h, pl.ds(CAP * g, CAP)], row_send.at[h, g], row_recv.at[h, g],
            device_id=(bins, at(x + dx, z + hop)), device_id_type=MESH,
        )

    def stays(g):
        return order[g][0] == 0 and order[g][2] == 0

    def box(job):
        return 0 if job > 0 else 1, abs(job) - 1

    def sum_copy(h, job, p):
        side, level = box(job)
        index = ((h * 2 + side) * LEVELS + level) * 4 + p
        return pltpu.make_async_remote_copy(
            acc.at[h, jobs.index(job), p], inbox.at[h, side, level, p], sum_send.at[index], sum_recv.at[index],
            device_id=(bins, at(x, z + (1 if job > 0 else -1))), device_id_type=MESH,
        )

    barrier = pltpu.get_barrier_semaphore()
    for step in range(1, NXZ):
        pl.semaphore_signal(barrier, inc=1, device_id=(bins, (site + step) % NXZ), device_id_type=MESH)
    for step in range(1, nbins):
        pl.semaphore_signal(barrier, inc=1, device_id=((bins + step) % nbins, site), device_id_type=MESH)

    fetches = [
        pltpu.make_async_copy(there, here, fetch_sem.at[i])
        for i, (there, here) in enumerate(
            ((owner_hbm, owner), (bin_hbm, local_bin), (moment_hbm, moment), (greens_hbm, rows))
        )
    ]
    for fetch in fetches:
        fetch.start()

    for fetch in fetches[:3]:
        fetch.wait()
    faults = owner.shape[1]
    fault = lax.broadcasted_iota(jnp.int32, (faults, LANES), 0)
    spot = lax.broadcasted_iota(jnp.int32, (faults, LANES), 1)
    square = (faults, faults)
    diagonal = lax.broadcasted_iota(jnp.int32, square, 0) == lax.broadcasted_iota(jnp.int32, square, 1)
    serving = jnp.sum(jnp.where(diagonal, owner[...], 0), axis=1, keepdims=True)
    wanted = jnp.sum(jnp.where(diagonal, local_bin[...] + 1, 0), axis=1, keepdims=True)
    hit = serving == spot % NXZ
    rank = hit.astype(jnp.int32)
    shift = 1
    while shift < faults:
        rank += jnp.concatenate([jnp.zeros((shift, LANES), jnp.int32), rank[:-shift]], axis=0)
        shift *= 2
    chosen = hit & (rank == spot // NXZ + 1)
    table = jnp.sum(jnp.where(chosen, wanted * 65536 + fault + 1, 0), axis=0, keepdims=True)
    table_out[...] = table
    tables[site] = table
    own_rate = jnp.concatenate([moment[0], jnp.zeros((faults, HALF), jnp.bfloat16)], axis=1)
    moment_out[...] = own_rate
    moments[bins] = own_rate

    pl.semaphore_wait(barrier, NXZ - 1 + nbins - 1)
    for step in range(1, NXZ):
        table_copy(step).start()
    all_tables(table_sem.at[1]).wait()
    to_smem = pltpu.make_async_copy(tables, table_smem, smem_sem)
    to_smem.start()
    to_smem.wait()
    fetches[3].wait()

    def pass_on(h, g):
        dx, dz, hop = order[g]
        asking = at(x + dx, z + dz)
        target = land if stays(g) else sent
        samples = part // 8 * LANES

        def gather(r, _):
            row = rows[jnp.maximum(table_smem[asking, 0, NXZ * r + site] // 65536 - 1, 0)]
            row = row[:, samples * h : samples * (h + 1)]
            target[h, CAP * g + r] = jnp.concatenate(
                [row[:, LANES * m : LANES * (m + 1)] for m in range(part // 8)], axis=0
            )
            return 0

        lax.fori_loop(0, CAP, gather, 0)
        if not stays(g):
            row_copy(h, g).start()

    for i, (h, g) in enumerate(sends):
        pass_on(h, g)
        if i == 8:
            for step in range(1, nbins):
                moment_copy(step).start()

    for g, (dx, dz, hop) in enumerate(order):
        asking = at(x, z - hop + dz)
        source = at(x - dx, z - hop)
        for r in range(CAP):
            left[CAP * g + r] = table_smem[asking, 0, NXZ * r + source] % 65536

    all_moments(moment_sem.at[1]).wait()
    for p in range(4):
        base[p] = moments[2 * p + 1].astype(jnp.float32) + pltpu.roll(
            moments[2 * p].astype(jnp.float32), HALF, 1
        )
    square = (LANES, LANES)
    lane = lax.broadcasted_iota(jnp.int32, square, 1)
    lag = lane - lax.broadcasted_iota(jnp.int32, square, 0)
    inside = ((lane < HALF) & (lag < 0) & (lag >= -HALF)) | ((lane >= HALF) & (lag >= 0) & (lag < HALF))
    toep[0] = jnp.zeros(toep.shape[1:], toep.dtype)

    @pl.loop(0, faults)
    def _(f):
        for p in range(4):
            spread = jnp.broadcast_to(base[p, pl.ds(f, 1), :], square)
            turned = pltpu.roll(spread, 0, 1, stride=1, stride_axis=0)
            toep[f + 1, :, LANES * p : LANES * (p + 1)] = jnp.where(inside, turned, 0.0).astype(jnp.bfloat16)

    early_lane = lax.broadcasted_iota(jnp.int32, (part, LANES), 1) < HALF

    def window(h, slot):
        now = land[h, slot]
        swapped = pltpu.roll(now.astype(jnp.float32), HALF, 1)
        if h == 0:
            edge = jnp.zeros((8, LANES), jnp.float32)
        else:
            edge = pltpu.roll(land[h - 1, slot].astype(jnp.float32)[part - 8 :], HALF, 1)
        before = jnp.concatenate([edge, swapped[: part - 8]], axis=0)
        return jnp.concatenate([jnp.where(early_lane, before, swapped).astype(jnp.bfloat16), now], axis=0)

    def own_sums(h, job):
        first, last = spans[job]
        size = min(last - first, 5)
        for start in range(first, last, size):
            for g in range(start, start + size):
                if not stays(g):
                    row_copy(h, g).wait_recv()
            slots = range(CAP * start, CAP * (start + size))
            for i, slot in enumerate(slots):
                windows[:, LANES * i : LANES * (i + 1)] = window(h, slot)
            tiles = jnp.concatenate([toep[left[slot]] for slot in slots], axis=0)
            c = jnp.dot(windows[:, : LANES * len(slots)], tiles, preferred_element_type=jnp.float32)
            for p in range(4):
                mine = c[:, LANES * p : LANES * (p + 1)]
                if start == first:
                    acc[h, jobs.index(job), p] = mine
                else:
                    acc[h, jobs.index(job), p] += mine

    def send_sums(h, job):
        for p in range(4):
            if abs(job) < LEVELS:
                further = job + (1 if job > 0 else -1)
                sum_copy(h, further, p).wait_recv()
                side, level = box(further)
                acc[h, jobs.index(job), p] += inbox[h, side, level, p]
            sum_copy(h, job, p).start()

    half = lax.broadcasted_iota(jnp.int32, (8, LANES), 1) < HALF

    def finish(h):
        for p in range(4):
            total = acc[h, jobs.index(0), p]
            for job in (1, -1):
                sum_copy(h, job, p).wait_recv()
                side, level = box(job)
                total = total + inbox[h, side, level, p]
            for m in range(part // 8):
                early = total[8 * m : 8 * m + 8]
                late = total[part + 8 * m : part + 8 * m + 8]
                start = part // 8 * LANES * h + LANES * m
                where = slice(start, start + LANES)
                out[0, 2 * p, :, where] = jnp.where(half, early, pltpu.roll(late, HALF, 1)).astype(out.dtype)
                out[0, 2 * p + 1, :, where] = jnp.where(half, pltpu.roll(early, HALF, 1), late).astype(out.dtype)

    for h in range(PARTS):
        for k in range(LEVELS, 0, -1):
            if k == 1 and h > 0:
                own_sums(h - 1, 0)
            for job in (k, -k):
                own_sums(h, job)
                if k == LEVELS:
                    send_sums(h, job)
            if k < LEVELS:
                for job in (k, -k):
                    send_sums(h, job)
    own_sums(PARTS - 1, 0)
    for h in range(PARTS):
        finish(h)

    all_tables(table_sem.at[0]).wait()
    all_moments(moment_sem.at[0]).wait()
    for h in range(PARTS):
        for g in range(len(order)):
            if not stays(g):
                row_copy(h, g).wait_send()
        for job in jobs:
            if job != 0:
                for p in range(4):
                    sum_copy(h, job, p).wait_send()


def local(greens, moment_rate, bin_owner, bin_local):
    bins, channels, samples = greens.shape
    nbins = lax.axis_size("bins")
    faults = moment_rate.shape[1]
    slots = NXZ * CAP
    part = samples // LANES * channels // PARTS
    vmem, dma = pltpu.VMEM, pltpu.SemaphoreType.DMA
    sums = 2 * LEVELS + 1
    return pl.pallas_call(
        kernel,
        out_shape=jax.ShapeDtypeStruct((1, nbins, channels, samples), jnp.bfloat16),
        in_specs=[pl.BlockSpec(memory_space=pltpu.HBM)] * 4,
        out_specs=pl.BlockSpec(memory_space=vmem),
        scratch_shapes=[
            vmem(moment_rate.shape, jnp.bfloat16),
            vmem(bin_local.shape, jnp.int32),
            vmem(bin_local.shape, jnp.int32),
            vmem((bins, channels, samples), jnp.bfloat16),
            vmem((PARTS, slots, part, LANES), jnp.bfloat16),
            vmem((PARTS, slots, part, LANES), jnp.bfloat16),
            vmem((faults + 1, LANES, 4 * LANES), jnp.bfloat16),
            vmem((4, faults, LANES), jnp.float32),
            vmem((nbins, faults, LANES), jnp.bfloat16),
            vmem((faults, LANES), jnp.bfloat16),
            vmem((1, LANES), jnp.int32),
            vmem((NXZ, 1, LANES), jnp.int32),
            pltpu.SMEM((NXZ, 1, LANES), jnp.int32),
            pltpu.SMEM((slots,), jnp.int32),
            vmem((2 * part, 5 * CAP * LANES), jnp.bfloat16),
            vmem((PARTS, sums, 4, 2 * part, LANES), jnp.float32),
            vmem((PARTS, 2, LEVELS, 4, 2 * part, LANES), jnp.float32),
            dma((4,)),
            dma,
            dma((2,)),
            dma((2,)),
            dma((PARTS, NXZ)),
            dma((PARTS, NXZ)),
            dma((PARTS * LEVELS * 8,)),
            dma((PARTS * LEVELS * 8,)),
        ],
        compiler_params=pltpu.CompilerParams(
            collective_id=0, has_side_effects=True, vmem_limit_bytes=64 * 2**20
        ),
        cost_estimate=pl.CostEstimate(
            flops=slots * 2 * 256 * 128 * 512, bytes_accessed=2 * greens.size, transcendentals=0
        ),
    )(greens, moment_rate, bin_owner.reshape(bin_local.shape), bin_local)


def solution(mesh):
    placed = (
        P("sites", None, None),
        P("bins", None, None),
        P(("bins", "sites"), None, None),
        P(("bins", "sites"), None),
    )
    return jax.shard_map(
        local,
        mesh=mesh,
        in_specs=placed,
        out_specs=P(("bins", "sites"), None, None, None),
        check_vma=False,
    )
```
